32 devices in a mesh: scan: 8 (over y, x, core), tile: 4 (over z).
Axes of the slice: x: 2, y: 2, z: 4, core: 2. Of those that a mesh axis runs over, the one named last changes fastest.
Arguments:
- pointing: bfloat16 [8, 2048, 2048], P('tile', 'scan'), may hold values from -0.125 to 0.125
- ground_bin: int32 [8, 2048], P('tile', 'scan'), may hold values from 0 to 23
- degrees: int32 [8], P('tile'), may hold values from 2 to 8
- lengths: int32 [8], P('tile'), may hold values from 1 to 2048, 10240 in all
- tile_lists: int32 [8, 16], P('tile'), may hold values from 0 to 31, as said below
- owner_map: int32 [32], replicated, may hold values from 0 to 3, as said below
Outputs:
- obs_matrix: float32 [4096, 4096], P('tile', 'scan')
The draws below stay inside these ranges and needn't reach their ends.
Inputs may be any that keep to these rules, and one draw needn't show every extreme that they name: `owner_map`: for each j < 8, entries j * 4 to (j + 1) * 4 - 1 hold every owner 0 to 3 once. `tile_lists`: in each row, entries j * 2 to (j + 1) * 2 - 1 are distinct tiles of j * 4 to (j + 1) * 4 - 1; over the 2 rows of one index of tile, every owner is named (through owner_map) by exactly 8 entries.
All inputs are finite; a program needn't handle non-finite values. No bound on the sum of `lengths` on one device may be relied on, other than what follows from the above.
Results may differ from the reference program's by a relative error of at most 0.0003.
Values may be sent and summed in bfloat16 or wider, within the bound.
A program may use at most 128 MiB of HBM per device.

```python
import math
import jax
import jax.numpy as jnp
import numpy as np
from jax import lax

TILE_PIX = 128
K = 16
SCAN_DEV = 2
DEG_MAX = 8
NGB = 24
NTPL = 32
NS = 2048
SCANS = 8
NTILE = 32
K_COL = 2
KP = 2048
N_SCAN = 8
N_TILE = 4


def owner_tables(key):
    base_key = jax.random.fold_in(key, 7)
    range_keys = jax.random.split(base_key, N_SCAN)
    return jax.vmap(lambda one_key: jax.random.permutation(one_key, N_TILE))(range_keys).astype(jnp.int32)


def draw_owner_map(key, part):
    return owner_tables(key).reshape(-1).astype(jnp.int32)


def draw_tile_lists(key, part):
    tables = owner_tables(key)
    inverse = jnp.argsort(tables, axis=1).astype(jnp.int32)
    device_keys = jax.random.split(jax.random.fold_in(key, 13), N_TILE)
    shuffles = jax.vmap(lambda one_key: jax.random.permutation(one_key, N_TILE))(device_keys).astype(jnp.int32)
    slots = jnp.arange(SCAN_DEV)[:, None] * K + jnp.arange(K)[None, :]
    owners = shuffles[:, slots % N_TILE]
    range_index = jnp.arange(K) // K_COL
    within = inverse[range_index[None, None, :], owners]
    tiles = range_index[None, None, :] * N_TILE + within
    return tiles.reshape(SCANS, K).astype(jnp.int32)


def with_ends(result, rng, least, top_value):
    extent = result.shape
    place = [jax.random.randint(jax.random.fold_in(rng, axis), (), 0, extent[axis]) for axis in range(len(extent))]
    result = result.at[tuple(place)].set(least)
    longest = extent.index(max(extent))
    place[longest] = (place[longest] + 1) % extent[longest]
    return result.at[tuple(place)].set(top_value)


def block_levels(stream_key, dims, shards, smallest, largest):
    def one(axis_at, blocks):
        draws = jax.random.uniform(jax.random.fold_in(jax.random.fold_in(stream_key, 6), axis_at), (blocks,), jnp.float32, smallest / len(shards), largest / len(shards))
        return jnp.repeat(jnp.exp(draws), dims[axis_at] // blocks).reshape((-1,) + (1,) * (len(dims) - axis_at - 1))

    factor_of = one(*shards[0])
    for cut in shards[1:]:
        factor_of = factor_of * one(*cut)
    return factor_of


def profile(count, total, most, skew):
    loads = [(1 << 20) // math.isqrt(grade ** skew) + 1 for grade in range(2, count + 1)]
    rest, holding = total - most - (count - 1), [1] * (count - 1)
    while rest > 0:
        movable = [i for i in range(count - 1) if holding[i] < most]
        mass, remaining = sum([loads[i] for i in movable]), rest
        for i in movable:
            addition = min(most - holding[i], max(1, remaining * loads[i] // mass), rest)
            holding[i] = holding[i] + addition
            rest = rest - addition
    return np.array([most] + holding)


def uneven_parts(rng, number_of, total, most, slope):
    if number_of == 2:
        one = jax.random.randint(rng, (), max(1, total - most), min(most, total - 1) + 1)
        return jnp.stack([one, total - one])
    sizes = jnp.asarray(profile(number_of, total, most, slope), jnp.int32)
    pairs = (number_of - 1) // 2
    donor, taker = sizes[1:1 + 2 * pairs:2], sizes[2:2 + 2 * pairs:2]
    room = jnp.minimum(donor - 1, most - taker)
    moved = jax.random.randint(jax.random.fold_in(rng, 1), (pairs,), 0, 1 << 20) % (room + 1)
    sizes = sizes.at[1:1 + 2 * pairs:2].set(donor - moved).at[2:2 + 2 * pairs:2].set(taker + moved)
    return sizes[jax.random.permutation(jax.random.fold_in(rng, 2), number_of)]


def noise(stream_key, dims, width, limit, shards=(), held_as=jnp.bfloat16):
    level = block_levels(stream_key, dims, shards, -0.22, 0.18) if shards else 1.0
    values = jax.random.normal(stream_key, dims, jnp.float32) * width * level
    return jnp.minimum(jnp.maximum(values, -limit), limit).astype(held_as)


def setup_inputs(seed: int = 0) -> dict:
    arg_keys = jax.random.split(jax.random.key(seed), 7)
    return {
        "pointing": noise(arg_keys[0], (SCANS, NS, KP), KP ** -0.5, 0.125, ((0, 4), (1, 8))),
        "ground_bin": with_ends(jax.random.randint(arg_keys[1], (SCANS, NS), 0, NGB), jax.random.fold_in(arg_keys[1], 1), 0, NGB - 1).astype(jnp.int32),
        "degrees": with_ends(jax.random.randint(arg_keys[2], (SCANS,), 2, DEG_MAX + 1), jax.random.fold_in(arg_keys[2], 1), 2, DEG_MAX).astype(jnp.int32),
        "lengths": uneven_parts(arg_keys[3], SCANS, SCANS * NS * 5 // 8, NS, 2).astype(jnp.int32),
        "tile_lists": draw_tile_lists(jax.random.fold_in(arg_keys[6], 71), 0),
        "owner_map": draw_owner_map(jax.random.fold_in(arg_keys[6], 71), 0),
    }


def build_templates(ground_row, first_row, length_one, degree_one):
    sample_rows = ground_row.shape[0]
    position = (first_row + jnp.arange(sample_rows)).astype(jnp.float32)
    length_value = length_one.astype(jnp.float32)
    inside = position < length_value
    coord = 2.0 * (position + 0.5) / length_value - 1.0
    columns = []
    previous = jnp.ones_like(coord)
    current = coord
    for degree in range(1, DEG_MAX + 1):
        keep = jnp.logical_and(inside, degree <= degree_one)
        columns.append(jnp.where(keep, current, jnp.float32(0.0)))
        following = ((2.0 * degree + 1.0) * coord * current - degree * previous) / (degree + 1.0)
        previous, current = (current, following)
    poly_part = jnp.stack(columns, axis=1)
    bins = jnp.logical_and(ground_row[:, None] == jnp.arange(NGB)[None, :], inside[:, None]).astype(jnp.float32)
    return jnp.concatenate([poly_part, bins], axis=1).astype(jnp.bfloat16)

def reference(pointing, ground_bin, degrees, lengths, tile_lists, owner_map):
    start_matrix = jnp.zeros((NTILE, TILE_PIX, NTILE, TILE_PIX), jnp.float32)

    def one_scan(matrix, inputs):
        point_one, ground_one, degree_one, length_one, tiles_one = inputs
        inside = jnp.arange(NS) < length_one
        masked = jnp.where(inside[:, None], point_one, jnp.zeros_like(point_one))
        template = build_templates(ground_one, 0, length_one, degree_one)
        masked_f = masked.astype(jnp.float32)
        template_f = template.astype(jnp.float32)
        highest = lax.Precision.HIGHEST
        gram = jnp.dot(masked_f.T, masked_f, precision=highest)
        projected = jnp.dot(template_f.T, masked_f, precision=highest)
        normal = jnp.dot(template_f.T, template_f, precision=highest) + jnp.eye(NTPL, dtype=jnp.float32)
        factor = jnp.linalg.cholesky(normal)
        whitened = jax.scipy.linalg.solve_triangular(factor, projected, lower=True)
        contrib = gram - jnp.dot(whitened.T, whitened, precision=highest)
        blocks = contrib.reshape(K, TILE_PIX, K, TILE_PIX).transpose(0, 2, 1, 3)
        row_blocks = owner_map[tiles_one] * N_SCAN + tiles_one // N_TILE
        matrix = matrix.at[row_blocks[:, None], :, tiles_one[None, :], :].add(blocks)
        return (matrix, None)
    final, unused = lax.scan(one_scan, start_matrix, (pointing, ground_bin, degrees, lengths, tile_lists))
    return final.reshape(NTILE * TILE_PIX, NTILE * TILE_PIX)
```

```python
import functools

import jax
import jax.numpy as jnp
from jax import lax
from jax.experimental import pallas as pl
from jax.experimental.pallas import tpu as pltpu
from jax.sharding import PartitionSpec as P

DEG_MAX = 8
NGB = 24
STEPS = 32.0
LIMIT = 32000.0
HIGH = lax.Precision.HIGHEST


def build_templates_t(ground_rows, lengths, degrees):
    sample_rows = ground_rows.shape[1]
    position = jnp.arange(sample_rows).astype(jnp.float32)
    length_value = lengths.astype(jnp.float32)[:, None]
    inside = position[None, :] < length_value
    coord = 2.0 * (position[None, :] + 0.5) / length_value - 1.0
    columns = []
    previous = jnp.ones_like(coord)
    current = coord
    for degree in range(1, DEG_MAX + 1):
        keep = jnp.logical_and(inside, (degree <= degrees)[:, None])
        columns.append(jnp.where(keep, current, jnp.float32(0.0)))
        following = ((2.0 * degree + 1.0) * coord * current - degree * previous) / (degree + 1.0)
        previous, current = (current, following)
    poly_part = jnp.stack(columns, axis=1)
    bins = jnp.logical_and(
        ground_rows[:, None, :] == jnp.arange(NGB)[None, :, None], inside[:, None, :]
    ).astype(jnp.float32)
    return jnp.concatenate([poly_part, bins], axis=1).astype(jnp.bfloat16)


def contrib_kernel(
    tile_pixels, k_cols, capacity, n_tile,
    order_ref, lengths_ref, place_ref,
    point_ref, own_ref, template_ref, linv_ref, out_ref, own_t, white_own, blocks, scales,
):
    scan, chunk = pl.program_id(0), pl.program_id(1)
    scan_count, chunk_count = pl.num_programs(0), pl.num_programs(1)
    samples, col_width = own_ref.shape[1:]
    chunk_width = point_ref.shape[2]
    per_chunk = chunk_width // tile_pixels
    contract_last = (((1,), (1,)), ((), ()))

    @pl.when(chunk == 0)
    def _():
        position = lax.broadcasted_iota(jnp.int32, (col_width, samples), 1)
        turned = own_ref[0].T
        own_t[...] = jnp.where(position < lengths_ref[scan], turned, jnp.zeros_like(turned))
        proj = lax.dot_general(
            own_t[...], template_ref[0], contract_last, preferred_element_type=jnp.float32
        )
        white_own[...] = lax.dot_general(
            proj, linv_ref[0], contract_last, precision=HIGH, preferred_element_type=jnp.float32
        )

    gram = jnp.dot(own_t[...], point_ref[0], preferred_element_type=jnp.float32)
    proj = jnp.dot(template_ref[0], point_ref[0], preferred_element_type=jnp.float32)
    white = jnp.dot(linv_ref[0], proj, precision=HIGH, preferred_element_type=jnp.float32)
    total = gram - jnp.dot(
        white_own[...], white, precision=HIGH, preferred_element_type=jnp.float32
    )
    first = (scan * chunk_count + chunk) * per_chunk
    for b in range(per_chunk):
        blocks[first + b] = total[:, b * tile_pixels : (b + 1) * tile_pixels]

    @pl.when(jnp.logical_and(scan == scan_count - 1, chunk == chunk_count - 1))
    def _():
        scales[...] = jnp.zeros_like(scales)
        for dest in range(n_tile):

            def one(item, carry):
                entry = order_ref[dest * capacity + item]
                for k in range(k_cols):
                    part = blocks[entry, k * tile_pixels : (k + 1) * tile_pixels, :]
                    top = jnp.max(jnp.abs(part), axis=0, keepdims=True)
                    level = jnp.ceil(jnp.log2(jnp.maximum(top, 1e-30) / LIMIT) * STEPS)
                    coded = jnp.round(part * jnp.exp2(level * (-1.0 / STEPS))).astype(jnp.int32)
                    row = pl.multiple_of((item * k_cols + k) * tile_pixels, tile_pixels)
                    out_ref[dest, pl.ds(row, tile_pixels), :] = coded.astype(jnp.int16)
                    scales[dest, pl.ds(item * k_cols + k, 1), :] = level
                return carry

            lax.fori_loop(0, capacity, one, 0)
            base = capacity * col_width
            out_ref[dest, base:, :] = scales[dest].astype(jnp.int32).astype(jnp.int16)


def place_kernel(
    tile_pixels, group, n_tile, scan_count, index_ref, recv_ref, out_ref, scales
):
    row = pl.program_id(0)
    base = group * tile_pixels

    @pl.when(row == 0)
    def _():
        for source in range(n_tile):
            level = recv_ref[source, base:, :].astype(jnp.float32)
            scales[source] = jnp.exp2(level * (1.0 / STEPS))

    for col in range(n_tile):
        total = jnp.zeros((tile_pixels, tile_pixels), jnp.float32)
        for source in range(n_tile):
            for scan in range(scan_count):
                found = index_ref[((row * n_tile + col) * n_tile + source) * scan_count + scan]
                slot = jnp.maximum(found, 0)
                start = pl.multiple_of(slot * tile_pixels, tile_pixels)
                part = recv_ref[source, pl.ds(start, tile_pixels), :].astype(jnp.float32)
                scale = scales[source, pl.ds(slot, 1), :] * (found >= 0).astype(jnp.float32)
                total = total + part * scale
        out_ref[:, col * tile_pixels : (col + 1) * tile_pixels] = total.T


def per_device(pointing, ground_bin, degrees, lengths, tile_lists, owner_map):
    scan_count, sample_rows, width = pointing.shape
    n_scan = lax.axis_size("scan")
    n_tile = lax.axis_size("tile")
    scan_index = lax.axis_index("scan")
    tile_index = lax.axis_index("tile")
    k_tiles = tile_lists.shape[1]
    k_cols = k_tiles // n_scan
    tile_pixels = width // k_tiles
    col_width = k_cols * tile_pixels
    template_cols = DEG_MAX + NGB
    samples = sample_rows * n_scan
    row_total = scan_count * k_tiles
    capacity = row_total // n_tile
    group = capacity * k_cols
    group_pad = -(-group // 16) * 16

    point_rows = lax.all_gather(pointing, "scan", axis=1, tiled=True)

    small = jnp.concatenate([ground_bin, tile_lists], axis=1)
    small = lax.all_gather(small, ("tile", "scan"), axis=0, tiled=False)
    small = small.reshape(n_tile, n_scan, scan_count, sample_rows + k_tiles)
    ground_rows = lax.dynamic_index_in_dim(small, tile_index, 0, keepdims=False)[:, :, :sample_rows]
    ground_rows = ground_rows.transpose(1, 0, 2).reshape(scan_count, samples)
    all_lists = small[:, 0, :, sample_rows:]

    template = build_templates_t(ground_rows, lengths, degrees)
    normal = jnp.einsum("stn,sun->stu", template, template, preferred_element_type=jnp.float32)
    normal = normal + jnp.eye(template_cols, dtype=jnp.float32)[None, :, :]
    factor = jnp.linalg.cholesky(normal)
    eye = jnp.broadcast_to(jnp.eye(template_cols, dtype=jnp.float32)[None], normal.shape)
    linv = jax.scipy.linalg.solve_triangular(factor, eye, lower=True)

    tiles = jnp.arange(owner_map.shape[0])
    owners_all = jnp.sum(
        jnp.where(all_lists[..., None] == tiles, owner_map, 0), axis=-1
    ).reshape(n_tile, row_total)
    before = jnp.arange(row_total)[:, None] > jnp.arange(row_total)[None, :]
    same = owners_all[:, :, None] == owners_all[:, None, :]
    rank = jnp.sum(jnp.logical_and(same, before[None]), axis=2)
    my_slot = lax.dynamic_index_in_dim(owners_all * capacity + rank, tile_index, 0, keepdims=False)
    order = jnp.sum(
        jnp.where(my_slot[None, :] == jnp.arange(row_total)[:, None], jnp.arange(row_total)[None, :], 0),
        axis=1,
    ).astype(jnp.int32)

    mine = (owners_all == tile_index).reshape(n_tile, scan_count, k_tiles)
    rank = rank.reshape(n_tile, scan_count, k_tiles)
    row_hit = jnp.logical_and(
        mine[None], (all_lists // n_tile)[None] == jnp.arange(n_scan)[:, None, None, None]
    )
    row_item = jnp.sum(jnp.where(row_hit, rank[None] + 1, 0), axis=-1)
    my_cols = lax.dynamic_slice_in_dim(all_lists, scan_index * k_cols, k_cols, 2) - scan_index * n_tile
    col_hit = my_cols[None] == jnp.arange(n_tile)[:, None, None, None]
    col_item = jnp.sum(jnp.where(col_hit, jnp.arange(k_cols) + 1, 0), axis=-1)
    found = jnp.where(
        jnp.logical_and(row_item[:, None] > 0, col_item[None] > 0),
        (row_item[:, None] - 1) * k_cols + col_item[None] - 1,
        -1,
    )
    index = found.reshape(-1).astype(jnp.int32)

    chunk_width = min(4 * tile_pixels, width)
    send = pl.pallas_call(
        functools.partial(contrib_kernel, tile_pixels, k_cols, capacity, n_tile),
        grid_spec=pltpu.PrefetchScalarGridSpec(
            num_scalar_prefetch=3,
            grid=(scan_count, width // chunk_width),
            in_specs=[
                pl.BlockSpec((1, samples, chunk_width), lambda s, c, o, l, j: (s, 0, c)),
                pl.BlockSpec((1, samples, col_width), lambda s, c, o, l, j: (s, 0, j[0])),
                pl.BlockSpec((1, template_cols, samples), lambda s, c, o, l, j: (s, 0, 0)),
                pl.BlockSpec((1, template_cols, template_cols), lambda s, c, o, l, j: (s, 0, 0)),
            ],
            out_specs=pl.BlockSpec(
                (n_tile, group * tile_pixels + group_pad, tile_pixels), lambda s, c, o, l, j: (0, 0, 0)
            ),
            scratch_shapes=[
                pltpu.VMEM((col_width, samples), jnp.bfloat16),
                pltpu.VMEM((col_width, template_cols), jnp.float32),
                pltpu.VMEM((row_total, col_width, tile_pixels), jnp.float32),
                pltpu.VMEM((n_tile, group_pad, tile_pixels), jnp.float32),
            ],
        ),
        out_shape=jax.ShapeDtypeStruct(
            (n_tile, group * tile_pixels + group_pad, tile_pixels), jnp.int16
        ),
        compiler_params=pltpu.CompilerParams(vmem_limit_bytes=48 * 1024 * 1024),
    )(order, lengths, scan_index[None].astype(jnp.int32), point_rows, point_rows, template, linv)

    recv = lax.all_to_all(send, "tile", split_axis=0, concat_axis=0, tiled=True)

    return pl.pallas_call(
        functools.partial(place_kernel, tile_pixels, group, n_tile, scan_count),
        grid_spec=pltpu.PrefetchScalarGridSpec(
            num_scalar_prefetch=1,
            grid=(n_scan,),
            in_specs=[pl.BlockSpec(recv.shape, lambda r, i: (0, 0, 0))],
            out_specs=pl.BlockSpec((tile_pixels, n_tile * tile_pixels), lambda r, i: (r, 0)),
            scratch_shapes=[pltpu.VMEM((n_tile, group_pad, tile_pixels), jnp.float32)],
        ),
        out_shape=jax.ShapeDtypeStruct((n_scan * tile_pixels, n_tile * tile_pixels), jnp.float32),
        compiler_params=pltpu.CompilerParams(vmem_limit_bytes=32 * 1024 * 1024),
    )(index, recv)


def solution(mesh):
    return jax.shard_map(
        per_device,
        mesh=mesh,
        in_specs=(
            P("tile", "scan", None),
            P("tile", "scan"),
            P("tile"),
            P("tile"),
            P("tile", None),
            P(),
        ),
        out_specs=P("tile", "scan"),
        check_vma=False,
    )
```

```python
import functools

import jax
import jax.numpy as jnp
from jax import lax
from jax.experimental import pallas as pl
from jax.experimental.pallas import tpu as pltpu
from jax.sharding import PartitionSpec as P

DEG_MAX = 8
NGB = 24
STEPS = 32.0
LIMIT = 32000.0
HIGH = lax.Precision.HIGHEST


def build_templates_t(ground_rows, lengths, degrees):
    sample_rows = ground_rows.shape[1]
    position = jnp.arange(sample_rows).astype(jnp.float32)
    length_value = lengths.astype(jnp.float32)[:, None]
    inside = position[None, :] < length_value
    coord = 2.0 * (position[None, :] + 0.5) / length_value - 1.0
    columns = []
    previous = jnp.ones_like(coord)
    current = coord
    for degree in range(1, DEG_MAX + 1):
        keep = jnp.logical_and(inside, (degree <= degrees)[:, None])
        columns.append(jnp.where(keep, current, jnp.float32(0.0)))
        following = ((2.0 * degree + 1.0) * coord * current - degree * previous) / (degree + 1.0)
        previous, current = (current, following)
    poly_part = jnp.stack(columns, axis=1)
    bins = jnp.logical_and(
        ground_rows[:, None, :] == jnp.arange(NGB)[None, :, None], inside[:, None, :]
    ).astype(jnp.float32)
    return jnp.concatenate([poly_part, bins], axis=1).astype(jnp.bfloat16)


def contrib_kernel(
    tile_pixels, lengths_ref, place_ref,
    point_ref, own_ref, template_ref, linv_ref, blocks_ref, own_t, white_own,
):
    chunk = pl.program_id(0)
    samples, col_width = own_ref.shape
    per_chunk = point_ref.shape[1] // tile_pixels
    contract_last = (((1,), (1,)), ((), ()))

    @pl.when(chunk == 0)
    def _():
        position = lax.broadcasted_iota(jnp.int32, (col_width, samples), 1)
        turned = own_ref[...].T
        own_t[...] = jnp.where(position < lengths_ref[0], turned, jnp.zeros_like(turned))
        proj = lax.dot_general(
            own_t[...], template_ref[...], contract_last, preferred_element_type=jnp.float32
        )
        white_own[...] = lax.dot_general(
            proj, linv_ref[...], contract_last, precision=HIGH, preferred_element_type=jnp.float32
        )

    gram = jnp.dot(own_t[...], point_ref[...], preferred_element_type=jnp.float32)
    proj = jnp.dot(template_ref[...], point_ref[...], preferred_element_type=jnp.float32)
    white = jnp.dot(linv_ref[...], proj, precision=HIGH, preferred_element_type=jnp.float32)
    total = gram - jnp.dot(
        white_own[...], white, precision=HIGH, preferred_element_type=jnp.float32
    )
    for b in range(per_chunk):
        blocks_ref[b] = total[:, b * tile_pixels : (b + 1) * tile_pixels]


def code_kernel(tile_pixels, k_cols, capacity, order_ref, *refs):
    *block_refs, out_ref, scales = refs
    k_tiles, col_width = block_refs[0].shape[:2]
    dest = pl.program_id(0)
    scales[...] = jnp.zeros_like(scales)
    for item in range(capacity):
        entry = order_ref[dest * capacity + item]
        scan, place = entry // k_tiles, entry % k_tiles
        for k in range(k_cols):
            rows = slice(k * tile_pixels, (k + 1) * tile_pixels)
            part = block_refs[0][place, rows, :]
            for other in range(1, len(block_refs)):
                part = jnp.where(scan == other, block_refs[other][place, rows, :], part)
            top = jnp.max(jnp.abs(part), axis=0, keepdims=True)
            level = jnp.ceil(jnp.log2(jnp.maximum(top, 1e-30) / LIMIT) * STEPS)
            coded = jnp.round(part * jnp.exp2(level * (-1.0 / STEPS))).astype(jnp.int32)
            slot = item * k_cols + k
            out_ref[0, slot * tile_pixels : (slot + 1) * tile_pixels, :] = coded.astype(jnp.int16)
            scales[slot : slot + 1, :] = level
    out_ref[0, capacity * col_width :, :] = scales[...].astype(jnp.int32).astype(jnp.int16)


def place_kernel(
    tile_pixels, group, n_tile, scan_count, index_ref, recv_ref, out_ref, scales
):
    row = pl.program_id(0)
    base = group * tile_pixels

    @pl.when(row == 0)
    def _():
        for source in range(n_tile):
            level = recv_ref[source, base:, :].astype(jnp.float32)
            scales[source] = jnp.exp2(level * (1.0 / STEPS))

    for col in range(n_tile):
        total = jnp.zeros((tile_pixels, tile_pixels), jnp.float32)
        for source in range(n_tile):
            for scan in range(scan_count):
                found = index_ref[((row * n_tile + col) * n_tile + source) * scan_count + scan]
                slot = jnp.maximum(found, 0)
                start = pl.multiple_of(slot * tile_pixels, tile_pixels)
                part = recv_ref[source, pl.ds(start, tile_pixels), :].astype(jnp.float32)
                scale = scales[source, pl.ds(slot, 1), :] * (found >= 0).astype(jnp.float32)
                total = total + part * scale
        out_ref[:, col * tile_pixels : (col + 1) * tile_pixels] = total.T


def per_device(pointing, ground_bin, degrees, lengths, tile_lists, owner_map):
    scan_count, sample_rows, width = pointing.shape
    n_scan = lax.axis_size("scan")
    n_tile = lax.axis_size("tile")
    scan_index = lax.axis_index("scan")
    tile_index = lax.axis_index("tile")
    k_tiles = tile_lists.shape[1]
    k_cols = k_tiles // n_scan
    tile_pixels = width // k_tiles
    col_width = k_cols * tile_pixels
    template_cols = DEG_MAX + NGB
    samples = sample_rows * n_scan
    row_total = scan_count * k_tiles
    capacity = row_total // n_tile
    group = capacity * k_cols
    group_pad = -(-group // 16) * 16

    small = jnp.concatenate([ground_bin, tile_lists], axis=1)
    small = lax.all_gather(small, ("tile", "scan"), axis=0, tiled=False)
    small, pointing = lax.optimization_barrier((small, pointing))
    point_rows = [
        lax.all_gather(pointing[s], "scan", axis=0, tiled=True) for s in range(scan_count)
    ]
    small = small.reshape(n_tile, n_scan, scan_count, sample_rows + k_tiles)
    ground_rows = lax.dynamic_index_in_dim(small, tile_index, 0, keepdims=False)[:, :, :sample_rows]
    ground_rows = ground_rows.transpose(1, 0, 2).reshape(scan_count, samples)
    all_lists = small[:, 0, :, sample_rows:]

    template = build_templates_t(ground_rows, lengths, degrees)
    normal = jnp.einsum("stn,sun->stu", template, template, preferred_element_type=jnp.float32)
    normal = normal + jnp.eye(template_cols, dtype=jnp.float32)[None, :, :]
    factor = jnp.linalg.cholesky(normal)
    eye = jnp.broadcast_to(jnp.eye(template_cols, dtype=jnp.float32)[None], normal.shape)
    linv = jax.scipy.linalg.solve_triangular(factor, eye, lower=True)

    tiles = jnp.arange(owner_map.shape[0])
    owners_all = jnp.sum(
        jnp.where(all_lists[..., None] == tiles, owner_map, 0), axis=-1
    ).reshape(n_tile, row_total)
    before = jnp.arange(row_total)[:, None] > jnp.arange(row_total)[None, :]
    same = owners_all[:, :, None] == owners_all[:, None, :]
    rank = jnp.sum(jnp.logical_and(same, before[None]), axis=2)
    my_slot = lax.dynamic_index_in_dim(owners_all * capacity + rank, tile_index, 0, keepdims=False)
    order = jnp.sum(
        jnp.where(my_slot[None, :] == jnp.arange(row_total)[:, None], jnp.arange(row_total)[None, :], 0),
        axis=1,
    ).astype(jnp.int32)

    mine = (owners_all == tile_index).reshape(n_tile, scan_count, k_tiles)
    rank = rank.reshape(n_tile, scan_count, k_tiles)
    row_hit = jnp.logical_and(
        mine[None], (all_lists // n_tile)[None] == jnp.arange(n_scan)[:, None, None, None]
    )
    row_item = jnp.sum(jnp.where(row_hit, rank[None] + 1, 0), axis=-1)
    my_cols = lax.dynamic_slice_in_dim(all_lists, scan_index * k_cols, k_cols, 2) - scan_index * n_tile
    col_hit = my_cols[None] == jnp.arange(n_tile)[:, None, None, None]
    col_item = jnp.sum(jnp.where(col_hit, jnp.arange(k_cols) + 1, 0), axis=-1)
    found = jnp.where(
        jnp.logical_and(row_item[:, None] > 0, col_item[None] > 0),
        (row_item[:, None] - 1) * k_cols + col_item[None] - 1,
        -1,
    )
    index = found.reshape(-1).astype(jnp.int32)

    chunk_width = min(4 * tile_pixels, width)
    place = scan_index[None].astype(jnp.int32)
    blocks = []
    for s in range(scan_count):
        one = pl.pallas_call(
            functools.partial(contrib_kernel, tile_pixels),
            grid_spec=pltpu.PrefetchScalarGridSpec(
                num_scalar_prefetch=2,
                grid=(width // chunk_width,),
                in_specs=[
                    pl.BlockSpec((samples, chunk_width), lambda c, l, j: (0, c)),
                    pl.BlockSpec((samples, col_width), lambda c, l, j: (0, j[0])),
                    pl.BlockSpec((template_cols, samples), lambda c, l, j: (0, 0)),
                    pl.BlockSpec((template_cols, template_cols), lambda c, l, j: (0, 0)),
                ],
                out_specs=pl.BlockSpec(
                    (chunk_width // tile_pixels, col_width, tile_pixels), lambda c, l, j: (c, 0, 0)
                ),
                scratch_shapes=[
                    pltpu.VMEM((col_width, samples), jnp.bfloat16),
                    pltpu.VMEM((col_width, template_cols), jnp.float32),
                ],
            ),
            out_shape=jax.ShapeDtypeStruct((k_tiles, col_width, tile_pixels), jnp.float32),
            compiler_params=pltpu.CompilerParams(vmem_limit_bytes=58 * 1024 * 1024),
            cost_estimate=pl.CostEstimate(
                flops=2 * samples * width * (col_width + template_cols),
                bytes_accessed=2 * samples * width + 4 * width * col_width,
                transcendentals=0,
            ),
        )(lengths[s : s + 1], place, point_rows[s], point_rows[s], template[s], linv[s])
        blocks.append(one)

    send_rows = group * tile_pixels + group_pad
    send = pl.pallas_call(
        functools.partial(code_kernel, tile_pixels, k_cols, capacity),
        grid_spec=pltpu.PrefetchScalarGridSpec(
            num_scalar_prefetch=1,
            grid=(n_tile,),
            in_specs=[pl.BlockSpec(b.shape, lambda d, o: (0, 0, 0)) for b in blocks],
            out_specs=pl.BlockSpec((1, send_rows, tile_pixels), lambda d, o: (d, 0, 0)),
            scratch_shapes=[pltpu.VMEM((group_pad, tile_pixels), jnp.float32)],
        ),
        out_shape=jax.ShapeDtypeStruct((n_tile, send_rows, tile_pixels), jnp.int16),
        compiler_params=pltpu.CompilerParams(vmem_limit_bytes=32 * 1024 * 1024),
    )(order, *blocks)

    recv = lax.all_to_all(send, "tile", split_axis=0, concat_axis=0, tiled=True)

    return pl.pallas_call(
        functools.partial(place_kernel, tile_pixels, group, n_tile, scan_count),
        grid_spec=pltpu.PrefetchScalarGridSpec(
            num_scalar_prefetch=1,
            grid=(n_scan,),
            in_specs=[pl.BlockSpec(recv.shape, lambda r, i: (0, 0, 0))],
            out_specs=pl.BlockSpec((tile_pixels, n_tile * tile_pixels), lambda r, i: (r, 0)),
            scratch_shapes=[pltpu.VMEM((n_tile, group_pad, tile_pixels), jnp.float32)],
        ),
        out_shape=jax.ShapeDtypeStruct((n_scan * tile_pixels, n_tile * tile_pixels), jnp.float32),
        compiler_params=pltpu.CompilerParams(vmem_limit_bytes=32 * 1024 * 1024),
    )(index, recv)


def solution(mesh):
    return jax.shard_map(
        per_device,
        mesh=mesh,
        in_specs=(
            P("tile", "scan", None),
            P("tile", "scan"),
            P("tile"),
            P("tile"),
            P("tile", None),
            P(),
        ),
        out_specs=P("tile", "scan"),
        check_vma=False,
    )
```

```python
import functools

import jax
import jax.numpy as jnp
from jax import lax
from jax.experimental import pallas as pl
from jax.experimental.pallas import tpu as pltpu
from jax.sharding import PartitionSpec as P

DEG_MAX = 8
NGB = 24
STEPS = 32.0
LIMIT = 32000.0
HIGH = lax.Precision.HIGHEST


def build_templates_t(ground_rows, lengths, degrees):
    sample_rows = ground_rows.shape[1]
    position = jnp.arange(sample_rows).astype(jnp.float32)
    length_value = lengths.astype(jnp.float32)[:, None]
    inside = position[None, :] < length_value
    coord = 2.0 * (position[None, :] + 0.5) / length_value - 1.0
    columns = []
    previous = jnp.ones_like(coord)
    current = coord
    for degree in range(1, DEG_MAX + 1):
        keep = jnp.logical_and(inside, (degree <= degrees)[:, None])
        columns.append(jnp.where(keep, current, jnp.float32(0.0)))
        following = ((2.0 * degree + 1.0) * coord * current - degree * previous) / (degree + 1.0)
        previous, current = (current, following)
    poly_part = jnp.stack(columns, axis=1)
    bins = jnp.logical_and(
        ground_rows[:, None, :] == jnp.arange(NGB)[None, :, None], inside[:, None, :]
    ).astype(jnp.float32)
    return jnp.concatenate([poly_part, bins], axis=1).astype(jnp.bfloat16)


PIECES = 4


def gather_kernel(
    n_scan, n_tile, point_ref, ground_ref, lists_ref, points_out, ground_out, lists_out,
    send_sem, recv_sem, ground_send, ground_recv, lists_send, lists_recv, local_sem,
):
    me = lax.axis_index("scan")
    layer = lax.axis_index("tile")
    rows = point_ref.shape[1]
    step = rows // PIECES
    sibling = me + 1 - 2 * lax.rem(me, 2)
    across_x = me + 2 - 4 * lax.rem(lax.div(me, 2), 2)
    across_y = me + 4 - 8 * lax.rem(lax.div(me, 4), 2)
    far = across_x + across_y - me

    barrier = pltpu.get_barrier_semaphore()
    for shift in range(1, n_scan):
        pl.semaphore_signal(
            barrier, inc=1, device_id={"scan": lax.rem(me + shift, n_scan)},
            device_id_type=pl.DeviceIdType.MESH,
        )
    for shift in range(1, n_tile):
        pl.semaphore_signal(
            barrier, inc=1, device_id={"tile": lax.rem(layer + shift, n_tile)},
            device_id_type=pl.DeviceIdType.MESH,
        )
    pl.semaphore_wait(barrier, n_scan + n_tile - 2)

    def block(ref, owner, half, piece):
        start = pl.multiple_of(owner * rows + piece * step, step)
        return ref.at[half, pl.ds(start, step), :]

    def send(kind, half, piece, owner, target):
        if kind in (0, 1, 3):
            source = point_ref.at[half, pl.ds(piece * step, step), :]
        else:
            source = block(points_out, owner, half, piece)
        copy = pltpu.make_async_remote_copy(
            src_ref=source,
            dst_ref=block(points_out, owner, half, piece),
            send_sem=send_sem.at[kind, half, piece],
            recv_sem=recv_sem.at[kind, half, piece],
            device_id={"scan": target},
            device_id_type=pl.DeviceIdType.MESH,
        )
        copy.start()
        copies[kind, half, piece] = copy

    copies = {}
    small = []
    for piece in range(PIECES):
        send(0, 0, piece, me, across_x)
        send(1, 1, piece, me, across_y)
    for shift in range(1, n_scan):
        copy = pltpu.make_async_remote_copy(
            src_ref=ground_ref, dst_ref=ground_out.at[me],
            send_sem=ground_send.at[shift], recv_sem=ground_recv.at[shift],
            device_id={"scan": lax.rem(me + shift, n_scan)},
            device_id_type=pl.DeviceIdType.MESH,
        )
        copy.start()
        small.append(copy)
    for shift in range(1, n_tile):
        copy = pltpu.make_async_remote_copy(
            src_ref=lists_ref, dst_ref=lists_out.at[layer],
            send_sem=lists_send.at[shift], recv_sem=lists_recv.at[shift],
            device_id={"tile": lax.rem(layer + shift, n_tile)},
            device_id_type=pl.DeviceIdType.MESH,
        )
        copy.start()
        small.append(copy)
    for piece in range(PIECES):
        send(0, 1, piece, me, across_x)
        send(1, 0, piece, me, across_y)
    for half in range(2):
        for piece in range(PIECES):
            send(3, half, piece, me, sibling)
    own = [
        pltpu.make_async_copy(
            point_ref, points_out.at[:, pl.ds(pl.multiple_of(me * rows, rows), rows), :], local_sem.at[0]
        ),
        pltpu.make_async_copy(ground_ref, ground_out.at[me], local_sem.at[1]),
        pltpu.make_async_copy(lists_ref, lists_out.at[layer], local_sem.at[2]),
    ]
    for copy in own:
        copy.start()

    for piece in range(PIECES):
        copies[0, 0, piece].wait_recv()
        send(2, 0, piece, across_x, across_y)
        copies[1, 1, piece].wait_recv()
        send(2, 1, piece, across_y, across_x)
        send(4, 0, piece, across_x, sibling)
        send(5, 1, piece, across_y, sibling)
    for piece in range(PIECES):
        copies[0, 1, piece].wait_recv()
        send(4, 1, piece, across_x, sibling)
        copies[1, 0, piece].wait_recv()
        send(5, 0, piece, across_y, sibling)
    for piece in range(PIECES):
        for half in range(2):
            copies[2, half, piece].wait_recv()
            send(6, half, piece, far, sibling)
    for kind in range(7):
        for half in range(2):
            for piece in range(PIECES):
                copies[kind, half, piece].wait_send()
                if kind >= 3:
                    copies[kind, half, piece].wait_recv()
    for copy in small:
        copy.wait()
    for copy in own:
        copy.wait()


def gather_plane(pointing, ground_bin, tile_lists, n_scan, n_tile):
    scan_count, rows, width = pointing.shape
    anywhere = pl.BlockSpec(memory_space=pl.ANY)
    semaphores = pltpu.SemaphoreType.DMA
    return pl.pallas_call(
        functools.partial(gather_kernel, n_scan, n_tile),
        in_specs=[anywhere] * 3,
        out_specs=[anywhere] * 3,
        out_shape=[
            jax.ShapeDtypeStruct((scan_count, rows * n_scan, width), pointing.dtype),
            jax.ShapeDtypeStruct((n_scan,) + ground_bin.shape, ground_bin.dtype),
            jax.ShapeDtypeStruct((n_tile,) + tile_lists.shape, tile_lists.dtype),
        ],
        scratch_shapes=[
            semaphores((7, 2, PIECES)),
            semaphores((7, 2, PIECES)),
            semaphores((n_scan,)),
            semaphores((n_scan,)),
            semaphores((n_tile,)),
            semaphores((n_tile,)),
            semaphores((3,)),
        ],
        compiler_params=pltpu.CompilerParams(collective_id=0, has_side_effects=True),
    )(pointing, ground_bin, tile_lists)


def contrib_kernel(
    tile_pixels, k_cols, capacity, n_tile,
    order_ref, lengths_ref, place_ref,
    point_ref, own_ref, template_ref, linv_ref, out_ref, own_t, white_own, blocks, scales,
):
    scan, chunk = pl.program_id(0), pl.program_id(1)
    scan_count, chunk_count = pl.num_programs(0), pl.num_programs(1)
    samples, col_width = own_ref.shape[1:]
    chunk_width = point_ref.shape[2]
    per_chunk = chunk_width // tile_pixels
    contract_last = (((1,), (1,)), ((), ()))

    @pl.when(chunk == 0)
    def _():
        position = lax.broadcasted_iota(jnp.int32, (col_width, samples), 1)
        turned = own_ref[0].T
        own_t[...] = jnp.where(position < lengths_ref[scan], turned, jnp.zeros_like(turned))
        proj = lax.dot_general(
            own_t[...], template_ref[0], contract_last, preferred_element_type=jnp.float32
        )
        white_own[...] = lax.dot_general(
            proj, linv_ref[0], contract_last, precision=HIGH, preferred_element_type=jnp.float32
        )

    gram = jnp.dot(own_t[...], point_ref[0], preferred_element_type=jnp.float32)
    proj = jnp.dot(template_ref[0], point_ref[0], preferred_element_type=jnp.float32)
    white = jnp.dot(linv_ref[0], proj, precision=HIGH, preferred_element_type=jnp.float32)
    total = gram - jnp.dot(
        white_own[...], white, precision=HIGH, preferred_element_type=jnp.float32
    )
    first = (scan * chunk_count + chunk) * per_chunk
    for b in range(per_chunk):
        blocks[first + b] = total[:, b * tile_pixels : (b + 1) * tile_pixels]

    @pl.when(jnp.logical_and(scan == scan_count - 1, chunk == chunk_count - 1))
    def _():
        scales[...] = jnp.zeros_like(scales)
        for dest in range(n_tile):

            def one(item, carry):
                entry = order_ref[dest * capacity + item]
                for k in range(k_cols):
                    part = blocks[entry, k * tile_pixels : (k + 1) * tile_pixels, :]
                    top = jnp.max(jnp.abs(part), axis=0, keepdims=True)
                    level = jnp.ceil(jnp.log2(jnp.maximum(top, 1e-30) / LIMIT) * STEPS)
                    coded = jnp.round(part * jnp.exp2(level * (-1.0 / STEPS))).astype(jnp.int32)
                    row = pl.multiple_of((item * k_cols + k) * tile_pixels, tile_pixels)
                    out_ref[dest, pl.ds(row, tile_pixels), :] = coded.astype(jnp.int16)
                    scales[dest, pl.ds(item * k_cols + k, 1), :] = level
                return carry

            lax.fori_loop(0, capacity, one, 0)
            base = capacity * col_width
            out_ref[dest, base:, :] = scales[dest].astype(jnp.int32).astype(jnp.int16)


def place_kernel(
    tile_pixels, group, n_tile, scan_count, index_ref, recv_ref, out_ref, scales
):
    row = pl.program_id(0)
    base = group * tile_pixels

    @pl.when(row == 0)
    def _():
        for source in range(n_tile):
            level = recv_ref[source, base:, :].astype(jnp.float32)
            scales[source] = jnp.exp2(level * (1.0 / STEPS))

    for col in range(n_tile):
        total = jnp.zeros((tile_pixels, tile_pixels), jnp.float32)
        for source in range(n_tile):
            for scan in range(scan_count):
                found = index_ref[((row * n_tile + col) * n_tile + source) * scan_count + scan]
                slot = jnp.maximum(found, 0)
                start = pl.multiple_of(slot * tile_pixels, tile_pixels)
                part = recv_ref[source, pl.ds(start, tile_pixels), :].astype(jnp.float32)
                scale = scales[source, pl.ds(slot, 1), :] * (found >= 0).astype(jnp.float32)
                total = total + part * scale
        out_ref[:, col * tile_pixels : (col + 1) * tile_pixels] = total.T


def per_device(pointing, ground_bin, degrees, lengths, tile_lists, owner_map):
    scan_count, sample_rows, width = pointing.shape
    n_scan = lax.axis_size("scan")
    n_tile = lax.axis_size("tile")
    scan_index = lax.axis_index("scan")
    tile_index = lax.axis_index("tile")
    k_tiles = tile_lists.shape[1]
    k_cols = k_tiles // n_scan
    tile_pixels = width // k_tiles
    col_width = k_cols * tile_pixels
    template_cols = DEG_MAX + NGB
    samples = sample_rows * n_scan
    row_total = scan_count * k_tiles
    capacity = row_total // n_tile
    group = capacity * k_cols
    group_pad = -(-group // 16) * 16

    if n_scan == 8 and scan_count == 2:
        point_rows, ground_rows, all_lists = gather_plane(
            pointing, ground_bin, tile_lists, n_scan, n_tile
        )
    else:
        point_rows = lax.all_gather(pointing, "scan", axis=1, tiled=True)
        ground_rows = lax.all_gather(ground_bin, "scan", axis=0, tiled=False)
        all_lists = lax.all_gather(tile_lists, "tile", axis=0, tiled=False)
    ground_rows = ground_rows.transpose(1, 0, 2).reshape(scan_count, samples)

    template = build_templates_t(ground_rows, lengths, degrees)
    normal = jnp.einsum("stn,sun->stu", template, template, preferred_element_type=jnp.float32)
    normal = normal + jnp.eye(template_cols, dtype=jnp.float32)[None, :, :]
    factor = jnp.linalg.cholesky(normal)
    eye = jnp.broadcast_to(jnp.eye(template_cols, dtype=jnp.float32)[None], normal.shape)
    linv = jax.scipy.linalg.solve_triangular(factor, eye, lower=True)

    tiles = jnp.arange(owner_map.shape[0])
    owners_all = jnp.sum(
        jnp.where(all_lists[..., None] == tiles, owner_map, 0), axis=-1
    ).reshape(n_tile, row_total)
    before = jnp.arange(row_total)[:, None] > jnp.arange(row_total)[None, :]
    same = owners_all[:, :, None] == owners_all[:, None, :]
    rank = jnp.sum(jnp.logical_and(same, before[None]), axis=2)
    my_slot = lax.dynamic_index_in_dim(owners_all * capacity + rank, tile_index, 0, keepdims=False)
    order = jnp.sum(
        jnp.where(my_slot[None, :] == jnp.arange(row_total)[:, None], jnp.arange(row_total)[None, :], 0),
        axis=1,
    ).astype(jnp.int32)

    mine = (owners_all == tile_index).reshape(n_tile, scan_count, k_tiles)
    rank = rank.reshape(n_tile, scan_count, k_tiles)
    row_hit = jnp.logical_and(
        mine[None], (all_lists // n_tile)[None] == jnp.arange(n_scan)[:, None, None, None]
    )
    row_item = jnp.sum(jnp.where(row_hit, rank[None] + 1, 0), axis=-1)
    my_cols = lax.dynamic_slice_in_dim(all_lists, scan_index * k_cols, k_cols, 2) - scan_index * n_tile
    col_hit = my_cols[None] == jnp.arange(n_tile)[:, None, None, None]
    col_item = jnp.sum(jnp.where(col_hit, jnp.arange(k_cols) + 1, 0), axis=-1)
    found = jnp.where(
        jnp.logical_and(row_item[:, None] > 0, col_item[None] > 0),
        (row_item[:, None] - 1) * k_cols + col_item[None] - 1,
        -1,
    )
    index = found.reshape(-1).astype(jnp.int32)

    chunk_width = min(4 * tile_pixels, width)
    send = pl.pallas_call(
        functools.partial(contrib_kernel, tile_pixels, k_cols, capacity, n_tile),
        grid_spec=pltpu.PrefetchScalarGridSpec(
            num_scalar_prefetch=3,
            grid=(scan_count, width // chunk_width),
            in_specs=[
                pl.BlockSpec((1, samples, chunk_width), lambda s, c, o, l, j: (s, 0, c)),
                pl.BlockSpec((1, samples, col_width), lambda s, c, o, l, j: (s, 0, j[0])),
                pl.BlockSpec((1, template_cols, samples), lambda s, c, o, l, j: (s, 0, 0)),
                pl.BlockSpec((1, template_cols, template_cols), lambda s, c, o, l, j: (s, 0, 0)),
            ],
            out_specs=pl.BlockSpec(
                (n_tile, group * tile_pixels + group_pad, tile_pixels), lambda s, c, o, l, j: (0, 0, 0)
            ),
            scratch_shapes=[
                pltpu.VMEM((col_width, samples), jnp.bfloat16),
                pltpu.VMEM((col_width, template_cols), jnp.float32),
                pltpu.VMEM((row_total, col_width, tile_pixels), jnp.float32),
                pltpu.VMEM((n_tile, group_pad, tile_pixels), jnp.float32),
            ],
        ),
        out_shape=jax.ShapeDtypeStruct(
            (n_tile, group * tile_pixels + group_pad, tile_pixels), jnp.int16
        ),
        compiler_params=pltpu.CompilerParams(vmem_limit_bytes=48 * 1024 * 1024),
    )(order, lengths, scan_index[None].astype(jnp.int32), point_rows, point_rows, template, linv)

    recv = lax.all_to_all(send, "tile", split_axis=0, concat_axis=0, tiled=True)

    return pl.pallas_call(
        functools.partial(place_kernel, tile_pixels, group, n_tile, scan_count),
        grid_spec=pltpu.PrefetchScalarGridSpec(
            num_scalar_prefetch=1,
            grid=(n_scan,),
            in_specs=[pl.BlockSpec(recv.shape, lambda r, i: (0, 0, 0))],
            out_specs=pl.BlockSpec((tile_pixels, n_tile * tile_pixels), lambda r, i: (r, 0)),
            scratch_shapes=[pltpu.VMEM((n_tile, group_pad, tile_pixels), jnp.float32)],
        ),
        out_shape=jax.ShapeDtypeStruct((n_scan * tile_pixels, n_tile * tile_pixels), jnp.float32),
        compiler_params=pltpu.CompilerParams(vmem_limit_bytes=32 * 1024 * 1024),
    )(index, recv)


def solution(mesh):
    return jax.shard_map(
        per_device,
        mesh=mesh,
        in_specs=(
            P("tile", "scan", None),
            P("tile", "scan"),
            P("tile"),
            P("tile"),
            P("tile", None),
            P(),
        ),
        out_specs=P("tile", "scan"),
        check_vma=False,
    )
```

```python
import functools

import jax
import jax.numpy as jnp
from jax import lax
from jax.experimental import pallas as pl
from jax.experimental.pallas import tpu as pltpu
from jax.sharding import PartitionSpec as P

DEG_MAX = 8
NGB = 24
STEPS = 32.0
LIMIT = 32000.0
HIGH = lax.Precision.HIGHEST


def build_templates_t(ground_rows, lengths, degrees):
    sample_rows = ground_rows.shape[1]
    position = jnp.arange(sample_rows).astype(jnp.float32)
    length_value = lengths.astype(jnp.float32)[:, None]
    inside = position[None, :] < length_value
    coord = 2.0 * (position[None, :] + 0.5) / length_value - 1.0
    columns = []
    previous = jnp.ones_like(coord)
    current = coord
    for degree in range(1, DEG_MAX + 1):
        keep = jnp.logical_and(inside, (degree <= degrees)[:, None])
        columns.append(jnp.where(keep, current, jnp.float32(0.0)))
        following = ((2.0 * degree + 1.0) * coord * current - degree * previous) / (degree + 1.0)
        previous, current = (current, following)
    poly_part = jnp.stack(columns, axis=1)
    bins = jnp.logical_and(
        ground_rows[:, None, :] == jnp.arange(NGB)[None, :, None], inside[:, None, :]
    ).astype(jnp.float32)
    return jnp.concatenate([poly_part, bins], axis=1).astype(jnp.bfloat16)


PIECES = 8


def gather_kernel(
    n_scan, n_tile, point_ref, ground_ref, lists_ref, points_out, ground_out, lists_out,
    send_sem, recv_sem, ground_send, ground_recv, lists_send, lists_recv, local_sem,
):
    me = lax.axis_index("scan")
    layer = lax.axis_index("tile")
    rows = point_ref.shape[1]
    step = rows // PIECES
    sibling = me + 1 - 2 * lax.rem(me, 2)
    across_x = me + 2 - 4 * lax.rem(lax.div(me, 2), 2)
    across_y = me + 4 - 8 * lax.rem(lax.div(me, 4), 2)
    far = across_x + across_y - me

    barrier = pltpu.get_barrier_semaphore()
    for shift in range(1, n_scan):
        pl.semaphore_signal(
            barrier, inc=1, device_id={"scan": lax.rem(me + shift, n_scan)},
            device_id_type=pl.DeviceIdType.MESH,
        )
    for shift in range(1, n_tile):
        pl.semaphore_signal(
            barrier, inc=1, device_id={"tile": lax.rem(layer + shift, n_tile)},
            device_id_type=pl.DeviceIdType.MESH,
        )
    pl.semaphore_wait(barrier, n_scan + n_tile - 2)

    def block(ref, owner, half, piece):
        start = pl.multiple_of(owner * rows + piece * step, step)
        return ref.at[half, pl.ds(start, step), :]

    def send(kind, half, piece, owner, target):
        if kind in (0, 1, 3):
            source = point_ref.at[half, pl.ds(piece * step, step), :]
        else:
            source = block(points_out, owner, half, piece)
        copy = pltpu.make_async_remote_copy(
            src_ref=source,
            dst_ref=block(points_out, owner, half, piece),
            send_sem=send_sem.at[kind, half, piece],
            recv_sem=recv_sem.at[kind, half, piece],
            device_id={"scan": target},
            device_id_type=pl.DeviceIdType.MESH,
        )
        copy.start()
        copies[kind, half, piece] = copy

    copies = {}
    small = []
    for piece in range(PIECES):
        send(0, 0, piece, me, across_x)
        send(1, 1, piece, me, across_y)
    for shift in range(1, n_scan):
        copy = pltpu.make_async_remote_copy(
            src_ref=ground_ref, dst_ref=ground_out.at[me],
            send_sem=ground_send.at[shift], recv_sem=ground_recv.at[shift],
            device_id={"scan": lax.rem(me + shift, n_scan)},
            device_id_type=pl.DeviceIdType.MESH,
        )
        copy.start()
        small.append(copy)
    for shift in range(1, n_tile):
        copy = pltpu.make_async_remote_copy(
            src_ref=lists_ref, dst_ref=lists_out.at[layer],
            send_sem=lists_send.at[shift], recv_sem=lists_recv.at[shift],
            device_id={"tile": lax.rem(layer + shift, n_tile)},
            device_id_type=pl.DeviceIdType.MESH,
        )
        copy.start()
        small.append(copy)
    for piece in range(PIECES):
        send(0, 1, piece, me, across_x)
        send(1, 0, piece, me, across_y)
    for half in range(2):
        for piece in range(PIECES):
            send(3, half, piece, me, sibling)
    own = [
        pltpu.make_async_copy(
            point_ref, points_out.at[:, pl.ds(pl.multiple_of(me * rows, rows), rows), :], local_sem.at[0]
        ),
        pltpu.make_async_copy(ground_ref, ground_out.at[me], local_sem.at[1]),
        pltpu.make_async_copy(lists_ref, lists_out.at[layer], local_sem.at[2]),
    ]
    for copy in own:
        copy.start()

    for piece in range(PIECES):
        copies[0, 0, piece].wait_recv()
        send(2, 0, piece, across_x, across_y)
        copies[1, 1, piece].wait_recv()
        send(2, 1, piece, across_y, across_x)
        send(4, 0, piece, across_x, sibling)
        send(5, 1, piece, across_y, sibling)
    for piece in range(PIECES):
        copies[0, 1, piece].wait_recv()
        send(4, 1, piece, across_x, sibling)
        copies[1, 0, piece].wait_recv()
        send(5, 0, piece, across_y, sibling)
    for piece in range(PIECES):
        for half in range(2):
            copies[2, half, piece].wait_recv()
            send(6, half, piece, far, sibling)
    for kind in range(7):
        for half in range(2):
            for piece in range(PIECES):
                copies[kind, half, piece].wait_send()
                if kind >= 3:
                    copies[kind, half, piece].wait_recv()
    for copy in small:
        copy.wait()
    for copy in own:
        copy.wait()


def gather_plane(pointing, ground_bin, tile_lists, n_scan, n_tile):
    scan_count, rows, width = pointing.shape
    anywhere = pl.BlockSpec(memory_space=pl.ANY)
    semaphores = pltpu.SemaphoreType.DMA
    return pl.pallas_call(
        functools.partial(gather_kernel, n_scan, n_tile),
        in_specs=[anywhere] * 3,
        out_specs=[anywhere] * 3,
        out_shape=[
            jax.ShapeDtypeStruct((scan_count, rows * n_scan, width), pointing.dtype),
            jax.ShapeDtypeStruct((n_scan,) + ground_bin.shape, ground_bin.dtype),
            jax.ShapeDtypeStruct((n_tile,) + tile_lists.shape, tile_lists.dtype),
        ],
        scratch_shapes=[
            semaphores((7, 2, PIECES)),
            semaphores((7, 2, PIECES)),
            semaphores((n_scan,)),
            semaphores((n_scan,)),
            semaphores((n_tile,)),
            semaphores((n_tile,)),
            semaphores((3,)),
        ],
        compiler_params=pltpu.CompilerParams(collective_id=0, has_side_effects=True),
    )(pointing, ground_bin, tile_lists)


def contrib_kernel(
    tile_pixels, k_cols, capacity, n_tile,
    order_ref, lengths_ref, place_ref,
    point_ref, own_ref, template_ref, linv_ref, out_ref, own_t, white_own, blocks, scales,
):
    scan, chunk = pl.program_id(0), pl.program_id(1)
    scan_count, chunk_count = pl.num_programs(0), pl.num_programs(1)
    samples, col_width = own_ref.shape[1:]
    chunk_width = point_ref.shape[2]
    per_chunk = chunk_width // tile_pixels
    contract_last = (((1,), (1,)), ((), ()))

    @pl.when(chunk == 0)
    def _():
        position = lax.broadcasted_iota(jnp.int32, (col_width, samples), 1)
        turned = own_ref[0].T
        own_t[...] = jnp.where(position < lengths_ref[scan], turned, jnp.zeros_like(turned))
        proj = lax.dot_general(
            own_t[...], template_ref[0], contract_last, preferred_element_type=jnp.float32
        )
        white_own[...] = lax.dot_general(
            proj, linv_ref[0], contract_last, precision=HIGH, preferred_element_type=jnp.float32
        )

    gram = jnp.dot(own_t[...], point_ref[0], preferred_element_type=jnp.float32)
    proj = jnp.dot(template_ref[0], point_ref[0], preferred_element_type=jnp.float32)
    white = jnp.dot(linv_ref[0], proj, precision=HIGH, preferred_element_type=jnp.float32)
    total = gram - jnp.dot(
        white_own[...], white, precision=HIGH, preferred_element_type=jnp.float32
    )
    first = (scan * chunk_count + chunk) * per_chunk
    for b in range(per_chunk):
        blocks[first + b] = total[:, b * tile_pixels : (b + 1) * tile_pixels]

    @pl.when(jnp.logical_and(scan == scan_count - 1, chunk == chunk_count - 1))
    def _():
        scales[...] = jnp.zeros_like(scales)
        for dest in range(n_tile):

            def one(item, carry):
                entry = order_ref[dest * capacity + item]
                for k in range(k_cols):
                    part = blocks[entry, k * tile_pixels : (k + 1) * tile_pixels, :]
                    top = jnp.max(jnp.abs(part), axis=0, keepdims=True)
                    level = jnp.ceil(jnp.log2(jnp.maximum(top, 1e-30) / LIMIT) * STEPS)
                    coded = jnp.round(part * jnp.exp2(level * (-1.0 / STEPS))).astype(jnp.int32)
                    row = pl.multiple_of((item * k_cols + k) * tile_pixels, tile_pixels)
                    out_ref[dest, pl.ds(row, tile_pixels), :] = coded.astype(jnp.int16)
                    scales[dest, pl.ds(item * k_cols + k, 1), :] = level
                return carry

            lax.fori_loop(0, capacity, one, 0)
            base = capacity * col_width
            out_ref[dest, base:, :] = scales[dest].astype(jnp.int32).astype(jnp.int16)


def place_kernel(
    tile_pixels, group, n_tile, scan_count, index_ref, recv_ref, out_ref, scales
):
    row = pl.program_id(0)
    base = group * tile_pixels

    @pl.when(row == 0)
    def _():
        for source in range(n_tile):
            level = recv_ref[source, base:, :].astype(jnp.float32)
            scales[source] = jnp.exp2(level * (1.0 / STEPS))

    for col in range(n_tile):
        total = jnp.zeros((tile_pixels, tile_pixels), jnp.float32)
        for source in range(n_tile):
            for scan in range(scan_count):
                found = index_ref[((row * n_tile + col) * n_tile + source) * scan_count + scan]
                slot = jnp.maximum(found, 0)
                start = pl.multiple_of(slot * tile_pixels, tile_pixels)
                part = recv_ref[source, pl.ds(start, tile_pixels), :].astype(jnp.float32)
                scale = scales[source, pl.ds(slot, 1), :] * (found >= 0).astype(jnp.float32)
                total = total + part * scale
        out_ref[:, col * tile_pixels : (col + 1) * tile_pixels] = total.T


def per_device(pointing, ground_bin, degrees, lengths, tile_lists, owner_map):
    scan_count, sample_rows, width = pointing.shape
    n_scan = lax.axis_size("scan")
    n_tile = lax.axis_size("tile")
    scan_index = lax.axis_index("scan")
    tile_index = lax.axis_index("tile")
    k_tiles = tile_lists.shape[1]
    k_cols = k_tiles // n_scan
    tile_pixels = width // k_tiles
    col_width = k_cols * tile_pixels
    template_cols = DEG_MAX + NGB
    samples = sample_rows * n_scan
    row_total = scan_count * k_tiles
    capacity = row_total // n_tile
    group = capacity * k_cols
    group_pad = -(-group // 16) * 16

    if n_scan == 8 and scan_count == 2:
        point_rows, ground_rows, all_lists = gather_plane(
            pointing, ground_bin, tile_lists, n_scan, n_tile
        )
    else:
        point_rows = lax.all_gather(pointing, "scan", axis=1, tiled=True)
        ground_rows = lax.all_gather(ground_bin, "scan", axis=0, tiled=False)
        all_lists = lax.all_gather(tile_lists, "tile", axis=0, tiled=False)
    ground_rows = ground_rows.transpose(1, 0, 2).reshape(scan_count, samples)

    template = build_templates_t(ground_rows, lengths, degrees)
    normal = jnp.einsum("stn,sun->stu", template, template, preferred_element_type=jnp.float32)
    normal = normal + jnp.eye(template_cols, dtype=jnp.float32)[None, :, :]
    factor = jnp.linalg.cholesky(normal)
    eye = jnp.broadcast_to(jnp.eye(template_cols, dtype=jnp.float32)[None], normal.shape)
    linv = jax.scipy.linalg.solve_triangular(factor, eye, lower=True)

    tiles = jnp.arange(owner_map.shape[0])
    owners_all = jnp.sum(
        jnp.where(all_lists[..., None] == tiles, owner_map, 0), axis=-1
    ).reshape(n_tile, row_total)
    before = jnp.arange(row_total)[:, None] > jnp.arange(row_total)[None, :]
    same = owners_all[:, :, None] == owners_all[:, None, :]
    rank = jnp.sum(jnp.logical_and(same, before[None]), axis=2)
    my_slot = lax.dynamic_index_in_dim(owners_all * capacity + rank, tile_index, 0, keepdims=False)
    order = jnp.sum(
        jnp.where(my_slot[None, :] == jnp.arange(row_total)[:, None], jnp.arange(row_total)[None, :], 0),
        axis=1,
    ).astype(jnp.int32)

    mine = (owners_all == tile_index).reshape(n_tile, scan_count, k_tiles)
    rank = rank.reshape(n_tile, scan_count, k_tiles)
    row_hit = jnp.logical_and(
        mine[None], (all_lists // n_tile)[None] == jnp.arange(n_scan)[:, None, None, None]
    )
    row_item = jnp.sum(jnp.where(row_hit, rank[None] + 1, 0), axis=-1)
    my_cols = lax.dynamic_slice_in_dim(all_lists, scan_index * k_cols, k_cols, 2) - scan_index * n_tile
    col_hit = my_cols[None] == jnp.arange(n_tile)[:, None, None, None]
    col_item = jnp.sum(jnp.where(col_hit, jnp.arange(k_cols) + 1, 0), axis=-1)
    found = jnp.where(
        jnp.logical_and(row_item[:, None] > 0, col_item[None] > 0),
        (row_item[:, None] - 1) * k_cols + col_item[None] - 1,
        -1,
    )
    index = found.reshape(-1).astype(jnp.int32)

    chunk_width = min(4 * tile_pixels, width)
    send = pl.pallas_call(
        functools.partial(contrib_kernel, tile_pixels, k_cols, capacity, n_tile),
        grid_spec=pltpu.PrefetchScalarGridSpec(
            num_scalar_prefetch=3,
            grid=(scan_count, width // chunk_width),
            in_specs=[
                pl.BlockSpec((1, samples, chunk_width), lambda s, c, o, l, j: (s, 0, c)),
                pl.BlockSpec((1, samples, col_width), lambda s, c, o, l, j: (s, 0, j[0])),
                pl.BlockSpec((1, template_cols, samples), lambda s, c, o, l, j: (s, 0, 0)),
                pl.BlockSpec((1, template_cols, template_cols), lambda s, c, o, l, j: (s, 0, 0)),
            ],
            out_specs=pl.BlockSpec(
                (n_tile, group * tile_pixels + group_pad, tile_pixels), lambda s, c, o, l, j: (0, 0, 0)
            ),
            scratch_shapes=[
                pltpu.VMEM((col_width, samples), jnp.bfloat16),
                pltpu.VMEM((col_width, template_cols), jnp.float32),
                pltpu.VMEM((row_total, col_width, tile_pixels), jnp.float32),
                pltpu.VMEM((n_tile, group_pad, tile_pixels), jnp.float32),
            ],
        ),
        out_shape=jax.ShapeDtypeStruct(
            (n_tile, group * tile_pixels + group_pad, tile_pixels), jnp.int16
        ),
        compiler_params=pltpu.CompilerParams(vmem_limit_bytes=48 * 1024 * 1024),
    )(order, lengths, scan_index[None].astype(jnp.int32), point_rows, point_rows, template, linv)

    recv = lax.all_to_all(send, "tile", split_axis=0, concat_axis=0, tiled=True)

    return pl.pallas_call(
        functools.partial(place_kernel, tile_pixels, group, n_tile, scan_count),
        grid_spec=pltpu.PrefetchScalarGridSpec(
            num_scalar_prefetch=1,
            grid=(n_scan,),
            in_specs=[pl.BlockSpec(recv.shape, lambda r, i: (0, 0, 0))],
            out_specs=pl.BlockSpec((tile_pixels, n_tile * tile_pixels), lambda r, i: (r, 0)),
            scratch_shapes=[pltpu.VMEM((n_tile, group_pad, tile_pixels), jnp.float32)],
        ),
        out_shape=jax.ShapeDtypeStruct((n_scan * tile_pixels, n_tile * tile_pixels), jnp.float32),
        compiler_params=pltpu.CompilerParams(vmem_limit_bytes=32 * 1024 * 1024),
    )(index, recv)


def solution(mesh):
    return jax.shard_map(
        per_device,
        mesh=mesh,
        in_specs=(
            P("tile", "scan", None),
            P("tile", "scan"),
            P("tile"),
            P("tile"),
            P("tile", None),
            P(),
        ),
        out_specs=P("tile", "scan"),
        check_vma=False,
    )
```

```python
import functools

import jax
import jax.numpy as jnp
from jax import lax
from jax.experimental import pallas as pl
from jax.experimental.pallas import tpu as pltpu
from jax.sharding import PartitionSpec as P

DEG_MAX = 8
NGB = 24
STEPS = 32.0
LIMIT = 32000.0
HIGH = lax.Precision.HIGHEST


def build_templates_t(ground_rows, lengths, degrees):
    sample_rows = ground_rows.shape[1]
    position = jnp.arange(sample_rows).astype(jnp.float32)
    length_value = lengths.astype(jnp.float32)[:, None]
    inside = position[None, :] < length_value
    coord = 2.0 * (position[None, :] + 0.5) / length_value - 1.0
    columns = []
    previous = jnp.ones_like(coord)
    current = coord
    for degree in range(1, DEG_MAX + 1):
        keep = jnp.logical_and(inside, (degree <= degrees)[:, None])
        columns.append(jnp.where(keep, current, jnp.float32(0.0)))
        following = ((2.0 * degree + 1.0) * coord * current - degree * previous) / (degree + 1.0)
        previous, current = (current, following)
    poly_part = jnp.stack(columns, axis=1)
    bins = jnp.logical_and(
        ground_rows[:, None, :] == jnp.arange(NGB)[None, :, None], inside[:, None, :]
    ).astype(jnp.float32)
    return jnp.concatenate([poly_part, bins], axis=1).astype(jnp.bfloat16)


PIECES = 4


def gather_kernel(
    n_scan, n_tile, point_ref, ground_ref, lists_ref, points_out, ground_out, lists_out,
    send_sem, recv_sem, ground_send, ground_recv, lists_send, lists_recv, local_sem,
):
    me = lax.axis_index("scan")
    layer = lax.axis_index("tile")
    rows = point_ref.shape[1]
    step = rows // PIECES
    sibling = me + 1 - 2 * lax.rem(me, 2)
    across_x = me + 2 - 4 * lax.rem(lax.div(me, 2), 2)
    across_y = me + 4 - 8 * lax.rem(lax.div(me, 4), 2)
    far = across_x + across_y - me

    barrier = pltpu.get_barrier_semaphore()
    for shift in range(1, n_scan):
        pl.semaphore_signal(
            barrier, inc=1, device_id={"scan": lax.rem(me + shift, n_scan)},
            device_id_type=pl.DeviceIdType.MESH,
        )
    for shift in range(1, n_tile):
        pl.semaphore_signal(
            barrier, inc=1, device_id={"tile": lax.rem(layer + shift, n_tile)},
            device_id_type=pl.DeviceIdType.MESH,
        )
    pl.semaphore_wait(barrier, n_scan + n_tile - 2)

    def block(ref, owner, half, piece):
        start = pl.multiple_of(owner * rows + piece * step, step)
        return ref.at[half, pl.ds(start, step), :]

    def send(kind, half, piece, owner, target):
        if kind in (0, 1, 3):
            source = point_ref.at[half, pl.ds(piece * step, step), :]
        else:
            source = block(points_out, owner, half, piece)
        copy = pltpu.make_async_remote_copy(
            src_ref=source,
            dst_ref=block(points_out, owner, half, piece),
            send_sem=send_sem.at[kind, half, piece],
            recv_sem=recv_sem.at[kind, half, piece],
            device_id={"scan": target},
            device_id_type=pl.DeviceIdType.MESH,
        )
        copy.start()
        copies[kind, half, piece] = copy

    copies = {}
    small = []
    for piece in range(PIECES):
        send(0, 0, piece, me, across_x)
        send(1, 1, piece, me, across_y)
    for shift in range(1, n_scan):
        copy = pltpu.make_async_remote_copy(
            src_ref=ground_ref, dst_ref=ground_out.at[me],
            send_sem=ground_send.at[shift], recv_sem=ground_recv.at[shift],
            device_id={"scan": lax.rem(me + shift, n_scan)},
            device_id_type=pl.DeviceIdType.MESH,
        )
        copy.start()
        small.append(copy)
    for shift in range(1, n_tile):
        copy = pltpu.make_async_remote_copy(
            src_ref=lists_ref, dst_ref=lists_out.at[layer],
            send_sem=lists_send.at[shift], recv_sem=lists_recv.at[shift],
            device_id={"tile": lax.rem(layer + shift, n_tile)},
            device_id_type=pl.DeviceIdType.MESH,
        )
        copy.start()
        small.append(copy)
    for piece in range(PIECES):
        send(0, 1, piece, me, across_x)
        send(1, 0, piece, me, across_y)
    for half in range(2):
        for piece in range(PIECES):
            send(3, half, piece, me, sibling)
    own = [
        pltpu.make_async_copy(
            point_ref, points_out.at[:, pl.ds(pl.multiple_of(me * rows, rows), rows), :], local_sem.at[0]
        ),
        pltpu.make_async_copy(ground_ref, ground_out.at[me], local_sem.at[1]),
        pltpu.make_async_copy(lists_ref, lists_out.at[layer], local_sem.at[2]),
    ]
    for copy in own:
        copy.start()

    for piece in range(PIECES):
        copies[0, 0, piece].wait_recv()
        send(2, 0, piece, across_x, across_y)
        copies[1, 1, piece].wait_recv()
        send(2, 1, piece, across_y, across_x)
        send(4, 0, piece, across_x, sibling)
        send(5, 1, piece, across_y, sibling)
    for piece in range(PIECES):
        copies[0, 1, piece].wait_recv()
        send(4, 1, piece, across_x, sibling)
        copies[1, 0, piece].wait_recv()
        send(5, 0, piece, across_y, sibling)
    for piece in range(PIECES):
        for half in range(2):
            copies[2, half, piece].wait_recv()
            send(6, half, piece, far, sibling)
    for kind in range(7):
        for half in range(2):
            for piece in range(PIECES):
                copies[kind, half, piece].wait_send()
                if kind >= 3:
                    copies[kind, half, piece].wait_recv()
    for copy in small:
        copy.wait()
    for copy in own:
        copy.wait()


def gather_plane(pointing, ground_bin, tile_lists, n_scan, n_tile):
    scan_count, rows, width = pointing.shape
    anywhere = pl.BlockSpec(memory_space=pl.ANY)
    semaphores = pltpu.SemaphoreType.DMA
    return pl.pallas_call(
        functools.partial(gather_kernel, n_scan, n_tile),
        in_specs=[anywhere] * 3,
        out_specs=[anywhere] * 3,
        out_shape=[
            jax.ShapeDtypeStruct((scan_count, rows * n_scan, width), pointing.dtype),
            jax.ShapeDtypeStruct((n_scan,) + ground_bin.shape, ground_bin.dtype),
            jax.ShapeDtypeStruct((n_tile,) + tile_lists.shape, tile_lists.dtype),
        ],
        scratch_shapes=[
            semaphores((7, 2, PIECES)),
            semaphores((7, 2, PIECES)),
            semaphores((n_scan,)),
            semaphores((n_scan,)),
            semaphores((n_tile,)),
            semaphores((n_tile,)),
            semaphores((3,)),
        ],
        compiler_params=pltpu.CompilerParams(collective_id=0, has_side_effects=True),
    )(pointing, ground_bin, tile_lists)


def contrib_kernel(
    tile_pixels, k_cols, capacity, n_tile,
    order_ref, lengths_ref, place_ref,
    point_ref, own_ref, template_ref, linv_ref, out_ref, own_t, white_own, blocks, scales,
):
    scan, chunk = pl.program_id(0), pl.program_id(1)
    scan_count, chunk_count = pl.num_programs(0), pl.num_programs(1)
    samples, col_width = own_ref.shape[1:]
    chunk_width = point_ref.shape[2]
    per_chunk = chunk_width // tile_pixels
    contract_last = (((1,), (1,)), ((), ()))

    @pl.when(chunk == 0)
    def _():
        position = lax.broadcasted_iota(jnp.int32, (col_width, samples), 1)
        turned = own_ref[0].T
        own_t[...] = jnp.where(position < lengths_ref[scan], turned, jnp.zeros_like(turned))
        proj = lax.dot_general(
            own_t[...], template_ref[0], contract_last, preferred_element_type=jnp.float32
        )
        white_own[...] = lax.dot_general(
            proj, linv_ref[0], contract_last, precision=HIGH, preferred_element_type=jnp.float32
        )

    gram = jnp.dot(own_t[...], point_ref[0], preferred_element_type=jnp.float32)
    proj = jnp.dot(template_ref[0], point_ref[0], preferred_element_type=jnp.float32)
    white = jnp.dot(linv_ref[0], proj, precision=HIGH, preferred_element_type=jnp.float32)
    total = gram - jnp.dot(
        white_own[...], white, precision=HIGH, preferred_element_type=jnp.float32
    )
    first = (scan * chunk_count + chunk) * per_chunk
    for b in range(per_chunk):
        blocks[first + b] = total[:, b * tile_pixels : (b + 1) * tile_pixels]

    @pl.when(jnp.logical_and(scan == scan_count - 1, chunk == chunk_count - 1))
    def _():
        scales[...] = jnp.zeros_like(scales)
        for dest in range(n_tile):

            def one(item, carry):
                entry = order_ref[dest * capacity + item]
                for k in range(k_cols):
                    part = blocks[entry, k * tile_pixels : (k + 1) * tile_pixels, :]
                    top = jnp.max(jnp.abs(part), axis=0, keepdims=True)
                    level = jnp.ceil(jnp.log2(jnp.maximum(top, 1e-30) / LIMIT) * STEPS)
                    coded = jnp.round(part * jnp.exp2(level * (-1.0 / STEPS))).astype(jnp.int32)
                    row = pl.multiple_of((item * k_cols + k) * tile_pixels, tile_pixels)
                    out_ref[dest, pl.ds(row, tile_pixels), :] = coded.astype(jnp.int16)
                    scales[dest, pl.ds(item * k_cols + k, 1), :] = level
                return carry

            lax.fori_loop(0, capacity, one, 0)
            base = capacity * col_width
            out_ref[dest, base:, :] = scales[dest].astype(jnp.int32).astype(jnp.int16)


def place_kernel(
    tile_pixels, group, n_tile, scan_count, index_ref, recv_ref, out_ref, scales
):
    row = pl.program_id(0)
    base = group * tile_pixels

    @pl.when(row == 0)
    def _():
        for source in range(n_tile):
            level = recv_ref[source, base:, :].astype(jnp.float32)
            scales[source] = jnp.exp2(level * (1.0 / STEPS))

    for col in range(n_tile):
        total = jnp.zeros((tile_pixels, tile_pixels), jnp.float32)
        for source in range(n_tile):
            for scan in range(scan_count):
                found = index_ref[((row * n_tile + col) * n_tile + source) * scan_count + scan]
                slot = jnp.maximum(found, 0)
                start = pl.multiple_of(slot * tile_pixels, tile_pixels)
                part = recv_ref[source, pl.ds(start, tile_pixels), :].astype(jnp.float32)
                scale = scales[source, pl.ds(slot, 1), :] * (found >= 0).astype(jnp.float32)
                total = total + part * scale
        out_ref[:, col * tile_pixels : (col + 1) * tile_pixels] = total.T


def per_device(pointing, ground_bin, degrees, lengths, tile_lists, owner_map):
    scan_count, sample_rows, width = pointing.shape
    n_scan = lax.axis_size("scan")
    n_tile = lax.axis_size("tile")
    scan_index = lax.axis_index("scan")
    tile_index = lax.axis_index("tile")
    k_tiles = tile_lists.shape[1]
    k_cols = k_tiles // n_scan
    tile_pixels = width // k_tiles
    col_width = k_cols * tile_pixels
    template_cols = DEG_MAX + NGB
    samples = sample_rows * n_scan
    row_total = scan_count * k_tiles
    capacity = row_total // n_tile
    group = capacity * k_cols
    group_pad = -(-group // 16) * 16

    if n_scan == 8 and scan_count == 2:
        point_rows, ground_rows, all_lists = gather_plane(
            pointing, ground_bin, tile_lists, n_scan, n_tile
        )
    else:
        point_rows = lax.all_gather(pointing, "scan", axis=1, tiled=True)
        ground_rows = lax.all_gather(ground_bin, "scan", axis=0, tiled=False)
        all_lists = lax.all_gather(tile_lists, "tile", axis=0, tiled=False)
    ground_rows = ground_rows.transpose(1, 0, 2).reshape(scan_count, samples)

    template = build_templates_t(ground_rows, lengths, degrees)
    normal = jnp.einsum("stn,sun->stu", template, template, preferred_element_type=jnp.float32)
    normal = normal + jnp.eye(template_cols, dtype=jnp.float32)[None, :, :]
    factor = jnp.linalg.cholesky(normal)
    eye = jnp.broadcast_to(jnp.eye(template_cols, dtype=jnp.float32)[None], normal.shape)
    linv = jax.scipy.linalg.solve_triangular(factor, eye, lower=True)

    tiles = jnp.arange(owner_map.shape[0])
    owners_all = jnp.sum(
        jnp.where(all_lists[..., None] == tiles, owner_map, 0), axis=-1
    ).reshape(n_tile, row_total)
    before = jnp.arange(row_total)[:, None] > jnp.arange(row_total)[None, :]
    same = owners_all[:, :, None] == owners_all[:, None, :]
    rank = jnp.sum(jnp.logical_and(same, before[None]), axis=2)
    my_slot = lax.dynamic_index_in_dim(owners_all * capacity + rank, tile_index, 0, keepdims=False)
    order = jnp.sum(
        jnp.where(my_slot[None, :] == jnp.arange(row_total)[:, None], jnp.arange(row_total)[None, :], 0),
        axis=1,
    ).astype(jnp.int32)

    mine = (owners_all == tile_index).reshape(n_tile, scan_count, k_tiles)
    rank = rank.reshape(n_tile, scan_count, k_tiles)
    row_hit = jnp.logical_and(
        mine[None], (all_lists // n_tile)[None] == jnp.arange(n_scan)[:, None, None, None]
    )
    row_item = jnp.sum(jnp.where(row_hit, rank[None] + 1, 0), axis=-1)
    my_cols = lax.dynamic_slice_in_dim(all_lists, scan_index * k_cols, k_cols, 2) - scan_index * n_tile
    col_hit = my_cols[None] == jnp.arange(n_tile)[:, None, None, None]
    col_item = jnp.sum(jnp.where(col_hit, jnp.arange(k_cols) + 1, 0), axis=-1)
    found = jnp.where(
        jnp.logical_and(row_item[:, None] > 0, col_item[None] > 0),
        (row_item[:, None] - 1) * k_cols + col_item[None] - 1,
        -1,
    )
    index = found.reshape(-1).astype(jnp.int32)

    chunk_width = min(8 * tile_pixels, width)
    send = pl.pallas_call(
        functools.partial(contrib_kernel, tile_pixels, k_cols, capacity, n_tile),
        grid_spec=pltpu.PrefetchScalarGridSpec(
            num_scalar_prefetch=3,
            grid=(scan_count, width // chunk_width),
            in_specs=[
                pl.BlockSpec((1, samples, chunk_width), lambda s, c, o, l, j: (s, 0, c)),
                pl.BlockSpec((1, samples, col_width), lambda s, c, o, l, j: (s, 0, j[0])),
                pl.BlockSpec((1, template_cols, samples), lambda s, c, o, l, j: (s, 0, 0)),
                pl.BlockSpec((1, template_cols, template_cols), lambda s, c, o, l, j: (s, 0, 0)),
            ],
            out_specs=pl.BlockSpec(
                (n_tile, group * tile_pixels + group_pad, tile_pixels), lambda s, c, o, l, j: (0, 0, 0)
            ),
            scratch_shapes=[
                pltpu.VMEM((col_width, samples), jnp.bfloat16),
                pltpu.VMEM((col_width, template_cols), jnp.float32),
                pltpu.VMEM((row_total, col_width, tile_pixels), jnp.float32),
                pltpu.VMEM((n_tile, group_pad, tile_pixels), jnp.float32),
            ],
        ),
        out_shape=jax.ShapeDtypeStruct(
            (n_tile, group * tile_pixels + group_pad, tile_pixels), jnp.int16
        ),
        compiler_params=pltpu.CompilerParams(vmem_limit_bytes=48 * 1024 * 1024),
    )(order, lengths, scan_index[None].astype(jnp.int32), point_rows, point_rows, template, linv)

    recv = lax.all_to_all(send, "tile", split_axis=0, concat_axis=0, tiled=True)

    return pl.pallas_call(
        functools.partial(place_kernel, tile_pixels, group, n_tile, scan_count),
        grid_spec=pltpu.PrefetchScalarGridSpec(
            num_scalar_prefetch=1,
            grid=(n_scan,),
            in_specs=[pl.BlockSpec(recv.shape, lambda r, i: (0, 0, 0))],
            out_specs=pl.BlockSpec((tile_pixels, n_tile * tile_pixels), lambda r, i: (r, 0)),
            scratch_shapes=[pltpu.VMEM((n_tile, group_pad, tile_pixels), jnp.float32)],
        ),
        out_shape=jax.ShapeDtypeStruct((n_scan * tile_pixels, n_tile * tile_pixels), jnp.float32),
        compiler_params=pltpu.CompilerParams(vmem_limit_bytes=32 * 1024 * 1024),
    )(index, recv)


def solution(mesh):
    return jax.shard_map(
        per_device,
        mesh=mesh,
        in_specs=(
            P("tile", "scan", None),
            P("tile", "scan"),
            P("tile"),
            P("tile"),
            P("tile", None),
            P(),
        ),
        out_specs=P("tile", "scan"),
        check_vma=False,
    )
```
